32 devices in a mesh: parts: 2 (over y), row: 2 (over core), col: 8 (over z, x).
Axes of the slice: x: 2, y: 2, z: 4, core: 2. Of those that a mesh axis runs over, the one named last changes fastest.
Arguments:
- hidden: bfloat16 [2048, 8192], P(('parts', 'row'), 'col'), parts along dimension 0, may hold values from -6 to 6
- target: bfloat16 [2048, 1024], P(('parts', 'col'), 'row'), parts along dimension 0, may hold values from -6 to 6
- v_weight: bfloat16 [16384, 1024], P(('parts', 'col'), 'row'), parts along dimension 0, may hold values from -0.0625 to 0.0625
- codes: int32 [16384, 1024], P(('parts', 'col'), 'row'), parts along dimension 0, may hold values from -8 to 7
- exponents: int32 [2048], P(('parts', 'row')), parts along dimension 0, may hold values from 7 to 10
- rotation: float32 [8192, 8192], P('col', 'row'), may hold values from -0.0625 to 0.0625
- head_rotation: float32 [256, 128], P('parts'), parts along dimension 0, may hold values from -0.5 to 0.5
Outputs:
- rotation_grad: float32 [16384, 8192], P(('parts', 'col'), 'row'), parts along dimension 0
- head_rotation_grad: float32 [256, 128], P('parts'), parts along dimension 0
The draws below stay inside these ranges and needn't reach their ends.
There are 2 independent parts, one for each index of `parts`. The reference program is written for one: setup_inputs(seed, part) draws one part's arguments, and reference() takes and returns one part's arrays. A program takes and returns all parts, laid end to end along the dimension named above; an argument that names none is the same for every part. Nothing has to cross between parts.
All inputs are finite; a program needn't handle non-finite values.
Results may differ from the reference program's by a relative error of at most 0.0059.
Values may be sent and summed in bfloat16 or wider, within the bound.
A program may use at most 192 MiB of HBM per device.

```python
import math
import jax
import jax.numpy as jnp
from jax import lax

D = 8192
KVH = 8
DH = 128
TOKENS = 1024
KV = 1024


def touch_ends(drawn, stream_key, smallest, top_value):
    longest = drawn.shape.index(max(drawn.shape))
    spots = []
    for shift in (0, 1):
        where = [jax.random.randint(jax.random.fold_in(stream_key, axis), (), 0, length) for axis, length in enumerate(drawn.shape)]
        where[longest] = (where[longest] + shift) % drawn.shape[longest]
        spots.append(tuple(where))
    return drawn.at[spots[0]].set(smallest).at[spots[1]].set(top_value)


def shard_levels(key, shape, pieces, least, high):
    loudness, own = 1.0, jax.random.fold_in(key, 6)
    for dim, blocks in pieces:
        steps = jnp.exp(jax.random.uniform(jax.random.fold_in(own, dim), (blocks,), jnp.float32, least / len(pieces), high / len(pieces)))
        loudness = loudness * jnp.repeat(steps, shape[dim] // blocks).reshape([-1 if axis == dim else 1 for axis in range(len(shape))])
    return loudness


def scatter_about(stream_key, shape, scale, limit, cuts=(), kind=jnp.bfloat16):
    values = jax.random.normal(stream_key, shape, jnp.float32) * scale
    if len(cuts) > 0:
        values = shard_levels(stream_key, shape, cuts, -0.22, 0.18) * values
    return jnp.clip(values, min=-limit, max=limit).astype(kind)


def setup_inputs(seed: int = 0, part: int = 0) -> dict:
    splits = jax.random.split(jax.random.key(seed), 8)
    own_keys = jax.random.split(jax.random.fold_in(splits[7], part), 8)
    hidden = scatter_about(own_keys[0], (TOKENS, D), 1.0, 6.0, ((0, 2), (1, 8)))
    target = scatter_about(own_keys[1], (TOKENS, KV), 1.0, 6.0, ((0, 8), (1, 2)))
    v_weight = scatter_about(own_keys[2], (D, KV), D ** -0.5, 0.0625, ((0, 8), (1, 2)))
    codes = touch_ends(jax.random.randint(own_keys[3], (D, KV), -8, 8), jax.random.fold_in(own_keys[3], 1), -8, 7).astype(jnp.int32)
    exponents = touch_ends(jax.random.randint(own_keys[4], (KV,), 7, 11), jax.random.fold_in(own_keys[4], 1), 7, 10).astype(jnp.int32)
    rotation = scatter_about(splits[5], (D, D), D ** -0.5, 0.0625, ((0, 8), (1, 2)), jnp.float32)
    head_rotation = scatter_about(own_keys[6], (DH, DH), DH ** -0.5, 0.5, (), jnp.float32)
    return {"hidden": hidden, "target": target, "v_weight": v_weight, "codes": codes, "exponents": exponents, "rotation": rotation, "head_rotation": head_rotation}


def reference(hidden, target, v_weight, codes, exponents, rotation, head_rotation):
    scales = jnp.exp2(-exponents.astype(jnp.float32))
    quantized = (codes.astype(jnp.float32) * scales[None, :]).astype(jnp.bfloat16)
    outputs = jnp.dot(hidden, quantized, preferred_element_type=jnp.float32)
    resid = ((outputs - target.astype(jnp.float32)) * (1.0 / math.sqrt(TOKENS))).astype(jnp.bfloat16)
    keep = jnp.where((codes > -8) & (codes < 7), 1.0, 0.0).astype(jnp.float32)
    weight_grad = lax.dot_general(hidden, resid, (((0,), (0,)), ((), ())), preferred_element_type=jnp.float32)
    grad_rot = (keep * weight_grad).astype(jnp.bfloat16)
    head_half = head_rotation.astype(jnp.bfloat16)
    rotated_w = jnp.dot(v_weight.reshape(D * KVH, DH), head_half, preferred_element_type=jnp.float32)
    rotated_w = rotated_w.reshape(D, KV).astype(jnp.bfloat16)
    rotation_grad = lax.dot_general(rotated_w, grad_rot, (((1,), (1,)), ((), ())), preferred_element_type=jnp.float32)
    carried = jnp.dot(rotation.astype(jnp.bfloat16), grad_rot, preferred_element_type=jnp.float32).astype(jnp.bfloat16)
    head_rotation_grad = lax.dot_general(v_weight.reshape(D * KVH, DH), carried.reshape(D * KVH, DH), (((0,), (0,)), ((), ())), preferred_element_type=jnp.float32)
    return (rotation_grad, head_rotation_grad)
```

```python
import math

import jax
import jax.numpy as jnp
from jax import lax
from jax.sharding import PartitionSpec as P

DH = 128


def on_device(hidden, target, v_weight, codes, exponents, rotation, head_rotation):
    cols = lax.axis_size("col")
    scales = jnp.exp2(-exponents.astype(jnp.float32))
    quantized = (codes.astype(jnp.float32) * scales[None, :]).astype(jnp.bfloat16)
    all_tokens = lax.all_gather(hidden, "row", axis=0, tiled=True)
    v_full = lax.all_gather(v_weight, "row", axis=1, tiled=True)
    token_count = all_tokens.shape[0]
    partial = jnp.dot(all_tokens, quantized, preferred_element_type=jnp.float32)
    pieces = partial.astype(jnp.bfloat16).reshape(cols, token_count // cols, -1)
    pieces = lax.all_to_all(pieces, "col", split_axis=0, concat_axis=0, tiled=True)
    outputs = jnp.sum(pieces.astype(jnp.float32), axis=0)
    resid = ((outputs - target.astype(jnp.float32)) * (1.0 / math.sqrt(token_count))).astype(
        jnp.bfloat16
    )
    weight_grad = lax.dot_general(
        all_tokens,
        lax.all_gather(resid, "col", axis=0, tiled=True),
        (((0,), (0,)), ((), ())),
        preferred_element_type=jnp.float32,
    )
    keep = jnp.where((codes > -8) & (codes < 7), 1.0, 0.0).astype(jnp.float32)
    grad_rot = (keep * weight_grad).astype(jnp.bfloat16)
    head_half = head_rotation.astype(jnp.bfloat16)
    rotated_w = jnp.dot(v_full.reshape(-1, DH), head_half, preferred_element_type=jnp.float32)
    rotated_w = rotated_w.reshape(v_full.shape).astype(jnp.bfloat16)
    stripe = lax.all_gather(grad_rot, "col", axis=0, tiled=True)
    stripe = lax.all_to_all(stripe, "row", split_axis=0, concat_axis=1, tiled=True)
    rotation_grad = lax.dot_general(
        rotated_w, stripe, (((1,), (1,)), ((), ())), preferred_element_type=jnp.float32
    )
    carried = jnp.dot(
        rotation.astype(jnp.bfloat16), stripe, preferred_element_type=jnp.float32
    ).astype(jnp.bfloat16)
    head_term = lax.dot_general(
        v_full.reshape(-1, DH),
        carried.reshape(-1, DH),
        (((0,), (0,)), ((), ())),
        preferred_element_type=jnp.float32,
    )
    head_rotation_grad = lax.psum(head_term, ("row", "col"))
    return (rotation_grad, head_rotation_grad)


def solution(mesh):
    in_specs = (
        P(("parts", "row"), "col"),
        P(("parts", "col"), "row"),
        P(("parts", "col"), "row"),
        P(("parts", "col"), "row"),
        P(("parts", "row")),
        P("col", "row"),
        P("parts", None),
    )
    out_specs = (P(("parts", "col"), "row"), P("parts", None))
    return jax.shard_map(
        on_device, mesh=mesh, in_specs=in_specs, out_specs=out_specs, check_vma=False
    )
```

```python
import functools
import math

import jax
import jax.numpy as jnp
from jax import lax
from jax.experimental import pallas as pl
from jax.experimental.pallas import tpu as pltpu
from jax.sharding import PartitionSpec as P

DH = 128
MESH = pl.DeviceIdType.MESH
F32 = jnp.float32
BF16 = jnp.bfloat16


def on_device(hidden, target, v_weight, codes, exponents, rotation, head_rotation):
    cols = lax.axis_size("col")
    scales = jnp.exp2(-exponents.astype(jnp.float32))
    quantized = (codes.astype(jnp.float32) * scales[None, :]).astype(jnp.bfloat16)
    all_tokens = lax.all_gather(hidden, "row", axis=0, tiled=True)
    v_full = lax.all_gather(v_weight, "row", axis=1, tiled=True)
    token_count = all_tokens.shape[0]
    partial = jnp.dot(all_tokens, quantized, preferred_element_type=jnp.float32)
    pieces = partial.astype(jnp.bfloat16).reshape(cols, token_count // cols, -1)
    pieces = lax.all_to_all(pieces, "col", split_axis=0, concat_axis=0, tiled=True)
    outputs = jnp.sum(pieces.astype(jnp.float32), axis=0)
    resid = ((outputs - target.astype(jnp.float32)) * (1.0 / math.sqrt(token_count))).astype(
        jnp.bfloat16
    )
    weight_grad = lax.dot_general(
        all_tokens,
        lax.all_gather(resid, "col", axis=0, tiled=True),
        (((0,), (0,)), ((), ())),
        preferred_element_type=jnp.float32,
    )
    keep = jnp.where((codes > -8) & (codes < 7), 1.0, 0.0).astype(jnp.float32)
    grad_rot = (keep * weight_grad).astype(jnp.bfloat16)
    head_half = head_rotation.astype(jnp.bfloat16)
    rotated_w = jnp.dot(v_full.reshape(-1, DH), head_half, preferred_element_type=jnp.float32)
    rotated_w = rotated_w.reshape(v_full.shape).astype(jnp.bfloat16)
    stripe = lax.all_gather(grad_rot, "col", axis=0, tiled=True)
    stripe = lax.all_to_all(stripe, "row", split_axis=0, concat_axis=1, tiled=True)
    rotation_grad = lax.dot_general(
        rotated_w, stripe, (((1,), (1,)), ((), ())), preferred_element_type=jnp.float32
    )
    carried = jnp.dot(
        rotation.astype(jnp.bfloat16), stripe, preferred_element_type=jnp.float32
    ).astype(jnp.bfloat16)
    head_term = lax.dot_general(
        v_full.reshape(-1, DH),
        carried.reshape(-1, DH),
        (((0,), (0,)), ((), ())),
        preferred_element_type=jnp.float32,
    )
    head_rotation_grad = lax.psum(head_term, ("row", "col"))
    return (rotation_grad, head_rotation_grad)


ZS = 4


def kernel(
    token_count,
    hidden,
    target,
    v_weight,
    codes,
    scales,
    head_half,
    rotation,
    rot_grad,
    head_grad,
    hid,
    vf,
    rw,
    part,
    part_own,
    arrived,
    resid,
    g_own,
    g_all,
    rot32,
    rot16,
    carried,
    stage,
    head_term,
    head_in,
    head_out,
    swap_send,
    swap_recv,
    rs_send,
    rs_recv,
    ag_own,
    ag_z,
    ag_x,
    ag_recv,
    g_src,
    g_z,
    g_x,
    g_recv,
    rot_sem,
    out_sem,
    hs_send,
    hs_recv,
    hb_send,
    hb_recv,
):
    r, c = lax.axis_index("row"), lax.axis_index("col")
    z, x = c // 2, c % 2
    me = c * 2 + r
    cols, people = 2 * ZS, 4 * ZS
    width, chans = codes.shape
    half_tokens = hidden.shape[0]
    piece = target.shape[0]
    tile = min(256, chans)
    wtile = min(256, width)

    def copy(src, dst, send, recv, cc, rr):
        return pltpu.make_async_remote_copy(
            src_ref=src,
            dst_ref=dst,
            send_sem=send,
            recv_sem=recv,
            device_id={"col": cc, "row": rr},
            device_id_type=MESH,
        )

    def rot_copy(b):
        return pltpu.make_async_copy(
            rotation.at[:, pl.ds(b * width, width)], rot32.at[b % 2], rot_sem.at[b]
        )

    rot_copy(0).start()
    rot_copy(1).start()

    barrier = pltpu.get_barrier_semaphore()
    for d in range(1, people):
        other = lax.rem(me + d, people)
        pl.semaphore_signal(
            barrier, inc=1, device_id={"col": other // 2, "row": other % 2}, device_id_type=MESH
        )
    pl.semaphore_wait(barrier, people - 1)

    swap_h = copy(hidden, hid.at[r], swap_send.at[0], swap_recv.at[0], c, 1 - r)
    swap_v = copy(v_weight, vf.at[r], swap_send.at[1], swap_recv.at[1], c, 1 - r)
    swap_h.start()
    swap_v.start()
    hid[r] = hidden[...]
    vf[r] = v_weight[...]

    quantized = (codes[...].astype(F32) * scales[...]).astype(BF16)

    def partial_half(h):
        product = jnp.dot(hid[h], quantized, preferred_element_type=F32)
        for i in range(ZS):
            owner = h * ZS + i
            rows = product[i * piece : (i + 1) * piece]
            part[owner] = rows.astype(BF16)

            @pl.when(owner == c)
            def _():
                part_own[...] = rows

        def send(i, carry):
            owner = h * ZS + lax.rem(c + i, ZS)

            @pl.when(owner != c)
            def _():
                copy(
                    part.at[owner], arrived.at[c], rs_send.at[owner], rs_recv.at[c], owner, r
                ).start()

            return carry

        lax.fori_loop(0, ZS, send, 0)

    partial_half(r)
    swap_h.wait_recv()
    partial_half(1 - r)

    def round_rotation(b):
        rot_copy(b).wait()

        def body(i, carry):
            rows = pl.ds(pl.multiple_of(i * 128, 128), 128)
            rot16[b, rows, :] = rot32[b % 2, rows, :].astype(BF16)
            return carry

        lax.fori_loop(0, width // 128, body, 0)
        if b + 2 < ZS:
            rot_copy(b + 2).start()

    round_rotation(0)
    round_rotation(1)
    swap_v.wait_recv()
    for k in range(2):
        for n in range(chans // DH):
            cut = slice(n * DH, (n + 1) * DH)
            rw[k, :, cut] = jnp.dot(
                vf[k, :, cut], head_half[...], preferred_element_type=F32
            ).astype(BF16)

    total = part_own[...] - target[...].astype(F32)
    for d in range(1, cols):
        s = lax.rem(c + d, cols)
        copy(part.at[s], arrived.at[s], rs_send.at[s], rs_recv.at[s], s, r).wait_recv()
        total = total + arrived[s].astype(F32)
    resid[c] = (total * (1.0 / math.sqrt(token_count))).astype(BF16)

    def ag_copy(s, sem, cc):
        return copy(resid.at[s], resid.at[s], sem, ag_recv.at[s], cc, r)

    def ag_first(act):
        @pl.when(z < ZS - 1)
        def _():
            act(ag_copy(c, ag_own.at[0], c + 2))

        @pl.when(z > 0)
        def _():
            act(ag_copy(c, ag_own.at[1], c - 2))

        act(ag_copy(c, ag_own.at[2], 2 * z + 1 - x))

    def ag_next(s, up, act):
        if up:

            @pl.when(z < ZS - 1)
            def _():
                act(ag_copy(s, ag_z.at[s], c + 2))

        else:

            @pl.when(z > 0)
            def _():
                act(ag_copy(s, ag_z.at[s], c - 2))

        act(ag_copy(s, ag_x.at[s], 2 * z + 1 - x))

    start = lambda cp: cp.start()
    sent = lambda cp: cp.wait_send()

    ag_first(start)
    round_rotation(2)
    for d in range(1, ZS):

        @pl.when(z >= d)
        def _():
            s = c - 2 * d
            ag_copy(s, ag_z.at[s], c).wait_recv()
            ag_next(s, True, start)

        @pl.when(z + d < ZS)
        def _():
            s = c + 2 * d
            ag_copy(s, ag_z.at[s], c).wait_recv()
            ag_next(s, False, start)

    round_rotation(3)
    for zz in range(ZS):
        s = 2 * zz + 1 - x
        ag_copy(s, ag_z.at[s], c).wait_recv()

    home = z // 2
    for n in range(chans // tile):
        cut = slice(n * tile, (n + 1) * tile)
        cot = resid[:, :, cut].reshape(token_count, tile)
        grad = lax.dot_general(
            hid[...].reshape(token_count, width),
            cot,
            (((0,), (0,)), ((), ())),
            preferred_element_type=F32,
        )
        kept = (codes[:, cut] > -8) & (codes[:, cut] < 7)
        g_own[:, cut] = jnp.where(kept, grad, 0.0).astype(BF16)

    def g_copy(src, slot, k, sem, cc, core):
        return copy(src, g_all.at[slot, k], sem, g_recv.at[slot * 2 + k], cc, core)

    mine = lax.rem(c, ZS)

    def g_first(act):
        @pl.when(z < ZS - 1)
        def _():
            act(g_copy(g_own, mine, r, g_src.at[0], c + 2, home))

        @pl.when(z > 0)
        def _():
            act(g_copy(g_own, mine, r, g_src.at[1], c - 2, home))

        act(g_copy(g_own, mine, r, g_src.at[2], 2 * z + 1 - x, home))

        @pl.when(r != home)
        def _():
            act(g_copy(g_own, mine, r, g_src.at[3], c, home))

    g_first(start)

    @pl.when(r == home)
    def _():
        g_all[mine, r] = g_own[...]

    def g_next(zs, k, act):
        slot = lax.rem(2 * zs + x, ZS)
        i = slot * 2 + k
        block = g_all.at[slot, k]

        @pl.when((zs < z) & (z < ZS - 1))
        def _():
            act(g_copy(block, slot, k, g_z.at[i], c + 2, r))

        @pl.when((zs > z) & (z > 0))
        def _():
            act(g_copy(block, slot, k, g_z.at[i], c - 2, r))

        @pl.when(zs != z)
        def _():
            act(g_copy(block, slot, k, g_x.at[i], 2 * z + 1 - x, r))

    near = jnp.clip(z, 2 * r, 2 * r + 1)
    far = 4 * r + 1 - near

    def out_copy(slot, n):
        return pltpu.make_async_copy(
            stage.at[n], rot_grad.at[:, pl.ds(pl.multiple_of(slot * width, 128), width)], out_sem.at[n]
        )

    def work(slot, n, first):
        if n >= 2:
            out_copy(slot, n % 2).wait()

        def outputs(i, carry):
            rows = pl.ds(pl.multiple_of(i * wtile, wtile), wtile)
            contract = (((1,), (1,)), ((), ()))
            stage[n % 2, :, rows] = lax.dot_general(
                rw[0], g_all[slot, 0, rows, :], contract, preferred_element_type=F32
            ) + lax.dot_general(
                rw[1], g_all[slot, 1, rows, :], contract, preferred_element_type=F32
            )
            return carry

        lax.fori_loop(0, width // wtile, outputs, 0)
        out_copy(slot, n % 2).start()

        def carry_on(i, carry):
            k = i // (chans // tile)
            cut = pl.ds(pl.multiple_of(lax.rem(i, chans // tile) * tile, tile), tile)
            product = jnp.dot(rot16[slot], g_all[slot, k, :, cut], preferred_element_type=F32)
            if first:
                carried[k, :, cut] = product
            else:
                carried[k, :, cut] += product
            return carry

        lax.fori_loop(0, 2 * (chans // tile), carry_on, 0)

    def g_wait(slot, k):
        copy(g_own, g_all.at[slot, k], g_src.at[0], g_recv.at[slot * 2 + k], c, r).wait_recv()

    n = 0
    for zs in (near, far):
        slot = lax.rem(2 * zs + x, ZS)
        for k in range(2):

            @pl.when((zs != z) | (r != k))
            def _():
                g_wait(slot, k)

            g_next(zs, k, start)
        work(slot, n, n == 0)
        n += 1
    for zs in (near, far):
        slot = lax.rem(2 * zs + 1 - x, ZS)
        for k in range(2):
            g_wait(slot, k)
        work(slot, n, False)
        n += 1

    term = jnp.zeros((DH, DH), F32)
    for k in range(2):
        for n in range(chans // DH):
            cut = slice(n * DH, (n + 1) * DH)
            term = term + lax.dot_general(
                vf[k, :, cut],
                carried[k, :, cut].astype(BF16),
                (((0,), (0,)), ((), ())),
                preferred_element_type=F32,
            )
    share = DH // people
    head_term[...] = term.reshape(people, share, DH)

    def hs_copy(d):
        other = lax.rem(me + d, people)
        return copy(
            head_term.at[other],
            head_in.at[me],
            hs_send.at[other],
            hs_recv.at[me],
            other // 2,
            other % 2,
        )

    def hb_copy(d):
        other = lax.rem(me + d, people)
        return copy(
            head_out.at[me],
            head_out.at[me],
            hb_send.at[other],
            hb_recv.at[me],
            other // 2,
            other % 2,
        )

    for d in range(1, people):
        hs_copy(d).start()
    total = head_term[me]
    for d in range(1, people):
        s = lax.rem(me + d, people)
        copy(head_in.at[s], head_in.at[s], hs_send.at[s], hs_recv.at[s], c, r).wait_recv()
        total = total + head_in[s]
    head_out[me] = total
    for d in range(1, people):
        hb_copy(d).start()
    for d in range(1, people):
        s = lax.rem(me + d, people)
        copy(head_out.at[s], head_out.at[s], hb_send.at[s], hb_recv.at[s], c, r).wait_recv()
    head_grad[...] = head_out[...].reshape(DH, DH)

    for d in range(1, people):
        hs_copy(d).wait_send()
        hb_copy(d).wait_send()
    swap_h.wait_send()
    swap_v.wait_send()
    for d in range(1, cols):
        s = lax.rem(c + d, cols)
        copy(part.at[s], arrived.at[c], rs_send.at[s], rs_recv.at[c], s, r).wait_send()
    ag_first(sent)
    for d in range(1, ZS):

        @pl.when(z >= d)
        def _():
            ag_next(c - 2 * d, True, sent)

        @pl.when(z + d < ZS)
        def _():
            ag_next(c + 2 * d, False, sent)

    g_first(sent)
    for zs in (near, far):
        for k in range(2):
            g_next(zs, k, sent)
    out_copy(0, 0).wait()
    out_copy(0, 1).wait()


def on_grid(hidden, target, v_weight, codes, exponents, rotation, head_rotation):
    width, chans = codes.shape
    piece = target.shape[0]
    cols, people = 2 * ZS, 4 * ZS
    token_count = 2 * hidden.shape[0]
    scales = jnp.exp2(-exponents.astype(F32))[None, :]
    head_half = head_rotation.astype(BF16)
    vmem = pl.BlockSpec(memory_space=pltpu.VMEM)
    anywhere = pl.BlockSpec(memory_space=pl.ANY)
    dma = pltpu.SemaphoreType.DMA
    return pl.pallas_call(
        functools.partial(kernel, token_count),
        out_shape=(
            jax.ShapeDtypeStruct(rotation.shape, F32),
            jax.ShapeDtypeStruct((DH, DH), F32),
        ),
        in_specs=[vmem] * 6 + [anywhere],
        out_specs=(anywhere, vmem),
        scratch_shapes=[
            pltpu.VMEM((2,) + hidden.shape, BF16),
            pltpu.VMEM((2, width, chans), BF16),
            pltpu.VMEM((2, width, chans), BF16),
            pltpu.VMEM((cols, piece, chans), BF16),
            pltpu.VMEM((piece, chans), F32),
            pltpu.VMEM((cols, piece, chans), BF16),
            pltpu.VMEM((cols, piece, chans), BF16),
            pltpu.VMEM((width, chans), BF16),
            pltpu.VMEM((ZS, 2, width, chans), BF16),
            pltpu.VMEM((2, width, width), F32),
            pltpu.VMEM((ZS, width, width), BF16),
            pltpu.VMEM((2, width, chans), F32),
            pltpu.VMEM((2, width, width), F32),
            pltpu.VMEM((people, DH // people, DH), F32),
            pltpu.VMEM((people, DH // people, DH), F32),
            pltpu.VMEM((people, DH // people, DH), F32),
            dma((2,)),
            dma((2,)),
            dma((cols,)),
            dma((cols,)),
            dma((3,)),
            dma((cols,)),
            dma((cols,)),
            dma((cols,)),
            dma((4,)),
            dma((cols,)),
            dma((cols,)),
            dma((cols,)),
            dma((ZS,)),
            dma((2,)),
            dma((people,)),
            dma((people,)),
            dma((people,)),
            dma((people,)),
        ],
        compiler_params=pltpu.CompilerParams(
            collective_id=0, has_side_effects=True, vmem_limit_bytes=62 * 1024 * 1024
        ),
    )(hidden, target, v_weight, codes, scales, head_half, rotation)


def solution(mesh):
    in_specs = (
        P(("parts", "row"), "col"),
        P(("parts", "col"), "row"),
        P(("parts", "col"), "row"),
        P(("parts", "col"), "row"),
        P(("parts", "row")),
        P("col", "row"),
        P("parts", None),
    )
    out_specs = (P(("parts", "col"), "row"), P("parts", None))
    routed = mesh.shape["col"] == 2 * ZS and mesh.shape["row"] == 2
    return jax.shard_map(
        on_grid if routed else on_device,
        mesh=mesh,
        in_specs=in_specs,
        out_specs=out_specs,
        check_vma=False,
    )
```

```python
import functools
import math

import jax
import jax.numpy as jnp
from jax import lax
from jax.experimental import pallas as pl
from jax.experimental.pallas import tpu as pltpu
from jax.sharding import PartitionSpec as P

DH = 128
MESH = pl.DeviceIdType.MESH
F32 = jnp.float32
BF16 = jnp.bfloat16


def on_device(hidden, target, v_weight, codes, exponents, rotation, head_rotation):
    cols = lax.axis_size("col")
    scales = jnp.exp2(-exponents.astype(jnp.float32))
    quantized = (codes.astype(jnp.float32) * scales[None, :]).astype(jnp.bfloat16)
    all_tokens = lax.all_gather(hidden, "row", axis=0, tiled=True)
    v_full = lax.all_gather(v_weight, "row", axis=1, tiled=True)
    token_count = all_tokens.shape[0]
    partial = jnp.dot(all_tokens, quantized, preferred_element_type=jnp.float32)
    pieces = partial.astype(jnp.bfloat16).reshape(cols, token_count // cols, -1)
    pieces = lax.all_to_all(pieces, "col", split_axis=0, concat_axis=0, tiled=True)
    outputs = jnp.sum(pieces.astype(jnp.float32), axis=0)
    resid = ((outputs - target.astype(jnp.float32)) * (1.0 / math.sqrt(token_count))).astype(
        jnp.bfloat16
    )
    weight_grad = lax.dot_general(
        all_tokens,
        lax.all_gather(resid, "col", axis=0, tiled=True),
        (((0,), (0,)), ((), ())),
        preferred_element_type=jnp.float32,
    )
    keep = jnp.where((codes > -8) & (codes < 7), 1.0, 0.0).astype(jnp.float32)
    grad_rot = (keep * weight_grad).astype(jnp.bfloat16)
    head_half = head_rotation.astype(jnp.bfloat16)
    rotated_w = jnp.dot(v_full.reshape(-1, DH), head_half, preferred_element_type=jnp.float32)
    rotated_w = rotated_w.reshape(v_full.shape).astype(jnp.bfloat16)
    stripe = lax.all_gather(grad_rot, "col", axis=0, tiled=True)
    stripe = lax.all_to_all(stripe, "row", split_axis=0, concat_axis=1, tiled=True)
    rotation_grad = lax.dot_general(
        rotated_w, stripe, (((1,), (1,)), ((), ())), preferred_element_type=jnp.float32
    )
    carried = jnp.dot(
        rotation.astype(jnp.bfloat16), stripe, preferred_element_type=jnp.float32
    ).astype(jnp.bfloat16)
    head_term = lax.dot_general(
        v_full.reshape(-1, DH),
        carried.reshape(-1, DH),
        (((0,), (0,)), ((), ())),
        preferred_element_type=jnp.float32,
    )
    head_rotation_grad = lax.psum(head_term, ("row", "col"))
    return (rotation_grad, head_rotation_grad)


ZS = 4


def kernel(
    token_count,
    hidden,
    target,
    v_weight,
    codes,
    scales,
    head_half,
    rotation,
    rot_grad,
    head_grad,
    hid,
    vf,
    rw,
    part,
    part_own,
    arrived,
    resid,
    g_own,
    g_all,
    rot32,
    vt,
    ut,
    head_sum,
    stage,
    head_term,
    head_in,
    head_out,
    swap_send,
    swap_recv,
    rs_send,
    rs_recv,
    ag_own,
    ag_z,
    ag_x,
    ag_recv,
    g_src,
    g_z,
    g_x,
    g_recv,
    rot_sem,
    out_sem,
    hs_send,
    hs_recv,
    hb_send,
    hb_recv,
):
    r, c = lax.axis_index("row"), lax.axis_index("col")
    z, x = c // 2, c % 2
    me = c * 2 + r
    cols, people = 2 * ZS, 4 * ZS
    width, chans = codes.shape
    half_tokens = hidden.shape[0]
    piece = target.shape[0]
    tile = min(256, chans)
    wtile = min(256, width)

    def copy(src, dst, send, recv, cc, rr):
        return pltpu.make_async_remote_copy(
            src_ref=src,
            dst_ref=dst,
            send_sem=send,
            recv_sem=recv,
            device_id={"col": cc, "row": rr},
            device_id_type=MESH,
        )

    def rot_copy(b):
        return pltpu.make_async_copy(
            rotation.at[:, pl.ds(b * width, width)], rot32.at[b % 2], rot_sem.at[b]
        )

    rot_copy(0).start()
    rot_copy(1).start()

    barrier = pltpu.get_barrier_semaphore()
    for d in range(1, people):
        other = lax.rem(me + d, people)
        pl.semaphore_signal(
            barrier, inc=1, device_id={"col": other // 2, "row": other % 2}, device_id_type=MESH
        )
    pl.semaphore_wait(barrier, people - 1)

    swap_h = copy(hidden, hid.at[r], swap_send.at[0], swap_recv.at[0], c, 1 - r)
    swap_v = copy(v_weight, vf.at[r], swap_send.at[1], swap_recv.at[1], c, 1 - r)
    swap_h.start()

    quantized = (codes[...].astype(F32) * scales[...]).astype(BF16)

    def partial_half(h, tokens):
        product = jnp.dot(tokens[...], quantized, preferred_element_type=F32)
        for i in range(ZS):
            owner = h * ZS + i
            rows = product[i * piece : (i + 1) * piece]
            part[owner] = rows.astype(BF16)

            @pl.when(owner == c)
            def _():
                part_own[...] = rows

        def send(i, carry):
            owner = h * ZS + lax.rem(c + i, ZS)

            @pl.when(owner != c)
            def _():
                copy(
                    part.at[owner], arrived.at[c], rs_send.at[owner], rs_recv.at[c], owner, r
                ).start()

            return carry

        lax.fori_loop(0, ZS, send, 0)

    partial_half(r, hidden)
    swap_h.wait_recv()
    swap_v.start()
    partial_half(1 - r, hid.at[1 - r])
    hid[r] = hidden[...]
    vf[r] = v_weight[...]

    def fold_rotation(b):
        rot_copy(b).wait()

        def body(i, carry):
            at = pl.ds(pl.multiple_of(i * wtile, wtile), wtile)
            ut[b, :, at] = jnp.dot(
                vt[...], rot32[b % 2, :, at].astype(BF16), preferred_element_type=F32
            ).astype(BF16)
            return carry

        lax.fori_loop(0, width // wtile, body, 0)
        if b + 2 < ZS:
            rot_copy(b + 2).start()

    swap_v.wait_recv()
    for k in range(2):
        vt[k * chans : (k + 1) * chans, :] = vf[k].T
    fold_rotation(0)
    fold_rotation(1)
    for k in range(2):
        for n in range(chans // DH):
            cut = slice(n * DH, (n + 1) * DH)
            rw[k, :, cut] = jnp.dot(
                vf[k, :, cut], head_half[...], preferred_element_type=F32
            ).astype(BF16)
    fold_rotation(2)

    total = part_own[...] - target[...].astype(F32)
    for d in range(1, cols):
        s = lax.rem(c + d, cols)
        copy(part.at[s], arrived.at[s], rs_send.at[s], rs_recv.at[s], s, r).wait_recv()
        total = total + arrived[s].astype(F32)
    resid[c] = (total * (1.0 / math.sqrt(token_count))).astype(BF16)

    def ag_copy(s, sem, cc):
        return copy(resid.at[s], resid.at[s], sem, ag_recv.at[s], cc, r)

    def ag_first(act):
        @pl.when(z < ZS - 1)
        def _():
            act(ag_copy(c, ag_own.at[0], c + 2))

        @pl.when(z > 0)
        def _():
            act(ag_copy(c, ag_own.at[1], c - 2))

        act(ag_copy(c, ag_own.at[2], 2 * z + 1 - x))

    def ag_next(s, up, act):
        if up:

            @pl.when(z < ZS - 1)
            def _():
                act(ag_copy(s, ag_z.at[s], c + 2))

        else:

            @pl.when(z > 0)
            def _():
                act(ag_copy(s, ag_z.at[s], c - 2))

        act(ag_copy(s, ag_x.at[s], 2 * z + 1 - x))

    start = lambda cp: cp.start()
    sent = lambda cp: cp.wait_send()

    ag_first(start)
    for d in range(1, ZS):

        @pl.when(z >= d)
        def _():
            s = c - 2 * d
            ag_copy(s, ag_z.at[s], c).wait_recv()
            ag_next(s, True, start)

        @pl.when(z + d < ZS)
        def _():
            s = c + 2 * d
            ag_copy(s, ag_z.at[s], c).wait_recv()
            ag_next(s, False, start)

    fold_rotation(3)
    for zz in range(ZS):
        s = 2 * zz + 1 - x
        ag_copy(s, ag_z.at[s], c).wait_recv()

    home = z // 2
    for n in range(chans // tile):
        cut = slice(n * tile, (n + 1) * tile)
        cot = resid[:, :, cut].reshape(token_count, tile)
        grad = lax.dot_general(
            hid[...].reshape(token_count, width),
            cot,
            (((0,), (0,)), ((), ())),
            preferred_element_type=F32,
        )
        kept = (codes[:, cut] > -8) & (codes[:, cut] < 7)
        g_own[:, cut] = jnp.where(kept, grad, 0.0).astype(BF16)

    def g_copy(src, slot, k, sem, cc, core):
        return copy(src, g_all.at[slot, k], sem, g_recv.at[slot * 2 + k], cc, core)

    mine = lax.rem(c, ZS)

    def g_first(act):
        @pl.when(z < ZS - 1)
        def _():
            act(g_copy(g_own, mine, r, g_src.at[0], c + 2, home))

        @pl.when(z > 0)
        def _():
            act(g_copy(g_own, mine, r, g_src.at[1], c - 2, home))

        act(g_copy(g_own, mine, r, g_src.at[2], 2 * z + 1 - x, home))

        @pl.when(r != home)
        def _():
            act(g_copy(g_own, mine, r, g_src.at[3], c, home))

    g_first(start)

    @pl.when(r == home)
    def _():
        g_all[mine, r] = g_own[...]

    def g_next(zs, k, act):
        slot = lax.rem(2 * zs + x, ZS)
        i = slot * 2 + k
        block = g_all.at[slot, k]

        @pl.when((zs < z) & (z < ZS - 1))
        def _():
            act(g_copy(block, slot, k, g_z.at[i], c + 2, r))

        @pl.when((zs > z) & (z > 0))
        def _():
            act(g_copy(block, slot, k, g_z.at[i], c - 2, r))

        crosses = zs != z
        if k == 1:
            crosses = crosses & (zs != end)

        @pl.when(crosses)
        def _():
            act(g_copy(block, slot, k, g_x.at[i], 2 * z + 1 - x, r))

    def g_beside(act):
        slot = lax.rem(2 * end + 1 - x, ZS)
        i = slot * 2 + 1

        @pl.when((r == 0) & (z < ZS - 1))
        def _():
            act(g_copy(g_all.at[slot, 1], slot, 1, g_z.at[i], c + 2, r))

        @pl.when((r == 1) & (z > 0))
        def _():
            act(g_copy(g_all.at[slot, 1], slot, 1, g_z.at[i], c - 2, r))

    end = (ZS - 1) * r
    near = jnp.clip(z, 2 * r, 2 * r + 1)
    far = 4 * r + 1 - near

    def out_copy(slot, n):
        return pltpu.make_async_copy(
            stage.at[n], rot_grad.at[:, pl.ds(pl.multiple_of(slot * width, 128), width)], out_sem.at[n]
        )

    def work(slot, n):
        if n >= 2:
            out_copy(slot, n % 2).wait()

        def outputs(i, carry):
            rows = pl.ds(pl.multiple_of(i * wtile, wtile), wtile)
            contract = (((1,), (1,)), ((), ()))
            stage[n % 2, :, rows] = lax.dot_general(
                rw[0], g_all[slot, 0, rows, :], contract, preferred_element_type=F32
            ) + lax.dot_general(
                rw[1], g_all[slot, 1, rows, :], contract, preferred_element_type=F32
            )
            return carry

        lax.fori_loop(0, width // wtile, outputs, 0)
        out_copy(slot, n % 2).start()

        pairs = chans // (2 * DH)

        def heads(i, carry):
            k = i // pairs
            rows = pl.ds(pl.multiple_of(i * 2 * DH, 2 * DH), 2 * DH)
            cut = pl.ds(pl.multiple_of(lax.rem(i, pairs) * 2 * DH, 2 * DH), 2 * DH)
            head_sum[...] += jnp.dot(
                ut[slot, rows, :], g_all[slot, k, :, cut], preferred_element_type=F32
            )
            return carry

        lax.fori_loop(0, 2 * pairs, heads, 0)

    def g_wait(slot, k):
        copy(g_own, g_all.at[slot, k], g_src.at[0], g_recv.at[slot * 2 + k], c, r).wait_recv()

    near_own, far_own = lax.rem(2 * near + x, ZS), lax.rem(2 * far + x, ZS)
    near_off, far_off = lax.rem(2 * near + 1 - x, ZS), lax.rem(2 * far + 1 - x, ZS)
    early = z + (ZS - 1) * r == ZS - 1

    head_sum[...] = jnp.zeros_like(head_sum)
    for k in range(2):

        @pl.when((near != z) | (r != k))
        def _():
            g_wait(near_own, k)

        g_next(near, k, start)
    work(near_own, 0)

    @pl.when(early)
    def _():
        g_wait(near_off, 0)
        g_wait(near_off, 1)
        work(near_off, 1)

    for k in range(2):
        g_wait(far_own, k)
        g_next(far, k, start)
    g_wait(lax.rem(2 * end + 1 - x, ZS), 1)
    g_beside(start)

    @pl.when(jnp.logical_not(early))
    def _():
        g_wait(near_off, 0)

        @pl.when(near != end)
        def _():
            g_wait(near_off, 1)

        work(near_off, 1)

    work(far_own, 2)
    g_wait(far_off, 0)

    @pl.when(far != end)
    def _():
        g_wait(far_off, 1)

    work(far_off, 3)

    term = head_sum[:DH, :DH] + head_sum[DH:, DH:]
    share = DH // people
    head_term[...] = term.reshape(people, share, DH)

    def hs_copy(d):
        other = lax.rem(me + d, people)
        return copy(
            head_term.at[other],
            head_in.at[me],
            hs_send.at[other],
            hs_recv.at[me],
            other // 2,
            other % 2,
        )

    def hb_copy(d):
        other = lax.rem(me + d, people)
        return copy(
            head_out.at[me],
            head_out.at[me],
            hb_send.at[other],
            hb_recv.at[me],
            other // 2,
            other % 2,
        )

    for d in range(1, people):
        hs_copy(d).start()
    total = head_term[me]
    for d in range(1, people):
        s = lax.rem(me + d, people)
        copy(head_in.at[s], head_in.at[s], hs_send.at[s], hs_recv.at[s], c, r).wait_recv()
        total = total + head_in[s]
    head_out[me] = total
    for d in range(1, people):
        hb_copy(d).start()
    for d in range(1, people):
        s = lax.rem(me + d, people)
        copy(head_out.at[s], head_out.at[s], hb_send.at[s], hb_recv.at[s], c, r).wait_recv()
    head_grad[...] = head_out[...].reshape(DH, DH)

    for d in range(1, people):
        hs_copy(d).wait_send()
        hb_copy(d).wait_send()
    swap_h.wait_send()
    swap_v.wait_send()
    for d in range(1, cols):
        s = lax.rem(c + d, cols)
        copy(part.at[s], arrived.at[c], rs_send.at[s], rs_recv.at[c], s, r).wait_send()
    ag_first(sent)
    for d in range(1, ZS):

        @pl.when(z >= d)
        def _():
            ag_next(c - 2 * d, True, sent)

        @pl.when(z + d < ZS)
        def _():
            ag_next(c + 2 * d, False, sent)

    g_first(sent)
    for zs in (near, far):
        for k in range(2):
            g_next(zs, k, sent)
    g_beside(sent)
    out_copy(0, 0).wait()
    out_copy(0, 1).wait()


def on_grid(hidden, target, v_weight, codes, exponents, rotation, head_rotation):
    width, chans = codes.shape
    piece = target.shape[0]
    cols, people = 2 * ZS, 4 * ZS
    token_count = 2 * hidden.shape[0]
    scales = jnp.exp2(-exponents.astype(F32))[None, :]
    head_half = head_rotation.astype(BF16)
    vmem = pl.BlockSpec(memory_space=pltpu.VMEM)
    anywhere = pl.BlockSpec(memory_space=pl.ANY)
    dma = pltpu.SemaphoreType.DMA
    return pl.pallas_call(
        functools.partial(kernel, token_count),
        out_shape=(
            jax.ShapeDtypeStruct(rotation.shape, F32),
            jax.ShapeDtypeStruct((DH, DH), F32),
        ),
        in_specs=[vmem] * 6 + [anywhere],
        out_specs=(anywhere, vmem),
        scratch_shapes=[
            pltpu.VMEM((2,) + hidden.shape, BF16),
            pltpu.VMEM((2, width, chans), BF16),
            pltpu.VMEM((2, width, chans), BF16),
            pltpu.VMEM((cols, piece, chans), BF16),
            pltpu.VMEM((piece, chans), F32),
            pltpu.VMEM((cols, piece, chans), BF16),
            pltpu.VMEM((cols, piece, chans), BF16),
            pltpu.VMEM((width, chans), BF16),
            pltpu.VMEM((ZS, 2, width, chans), BF16),
            pltpu.VMEM((2, width, width), F32),
            pltpu.VMEM((2 * chans, width), BF16),
            pltpu.VMEM((ZS, 2 * chans, width), BF16),
            pltpu.VMEM((2 * DH, 2 * DH), F32),
            pltpu.VMEM((2, width, width), F32),
            pltpu.VMEM((people, DH // people, DH), F32),
            pltpu.VMEM((people, DH // people, DH), F32),
            pltpu.VMEM((people, DH // people, DH), F32),
            dma((2,)),
            dma((2,)),
            dma((cols,)),
            dma((cols,)),
            dma((3,)),
            dma((cols,)),
            dma((cols,)),
            dma((cols,)),
            dma((4,)),
            dma((cols,)),
            dma((cols,)),
            dma((cols,)),
            dma((ZS,)),
            dma((2,)),
            dma((people,)),
            dma((people,)),
            dma((people,)),
            dma((people,)),
        ],
        compiler_params=pltpu.CompilerParams(
            collective_id=0, has_side_effects=True, vmem_limit_bytes=62 * 1024 * 1024
        ),
    )(hidden, target, v_weight, codes, scales, head_half, rotation)


def solution(mesh):
    in_specs = (
        P(("parts", "row"), "col"),
        P(("parts", "col"), "row"),
        P(("parts", "col"), "row"),
        P(("parts", "col"), "row"),
        P(("parts", "row")),
        P("col", "row"),
        P("parts", None),
    )
    out_specs = (P(("parts", "col"), "row"), P("parts", None))
    routed = mesh.shape["col"] == 2 * ZS and mesh.shape["row"] == 2
    return jax.shard_map(
        on_grid if routed else on_device,
        mesh=mesh,
        in_specs=in_specs,
        out_specs=out_specs,
        check_vma=False,
    )
```

```python
import functools
import math

import jax
import jax.numpy as jnp
from jax import lax
from jax.experimental import pallas as pl
from jax.experimental.pallas import tpu as pltpu
from jax.sharding import PartitionSpec as P

DH = 128
MESH = pl.DeviceIdType.MESH
F32 = jnp.float32
BF16 = jnp.bfloat16


def on_device(hidden, target, v_weight, codes, exponents, rotation, head_rotation):
    cols = lax.axis_size("col")
    scales = jnp.exp2(-exponents.astype(jnp.float32))
    quantized = (codes.astype(jnp.float32) * scales[None, :]).astype(jnp.bfloat16)
    all_tokens = lax.all_gather(hidden, "row", axis=0, tiled=True)
    v_full = lax.all_gather(v_weight, "row", axis=1, tiled=True)
    token_count = all_tokens.shape[0]
    partial = jnp.dot(all_tokens, quantized, preferred_element_type=jnp.float32)
    pieces = partial.astype(jnp.bfloat16).reshape(cols, token_count // cols, -1)
    pieces = lax.all_to_all(pieces, "col", split_axis=0, concat_axis=0, tiled=True)
    outputs = jnp.sum(pieces.astype(jnp.float32), axis=0)
    resid = ((outputs - target.astype(jnp.float32)) * (1.0 / math.sqrt(token_count))).astype(
        jnp.bfloat16
    )
    weight_grad = lax.dot_general(
        all_tokens,
        lax.all_gather(resid, "col", axis=0, tiled=True),
        (((0,), (0,)), ((), ())),
        preferred_element_type=jnp.float32,
    )
    keep = jnp.where((codes > -8) & (codes < 7), 1.0, 0.0).astype(jnp.float32)
    grad_rot = (keep * weight_grad).astype(jnp.bfloat16)
    head_half = head_rotation.astype(jnp.bfloat16)
    rotated_w = jnp.dot(v_full.reshape(-1, DH), head_half, preferred_element_type=jnp.float32)
    rotated_w = rotated_w.reshape(v_full.shape).astype(jnp.bfloat16)
    stripe = lax.all_gather(grad_rot, "col", axis=0, tiled=True)
    stripe = lax.all_to_all(stripe, "row", split_axis=0, concat_axis=1, tiled=True)
    rotation_grad = lax.dot_general(
        rotated_w, stripe, (((1,), (1,)), ((), ())), preferred_element_type=jnp.float32
    )
    carried = jnp.dot(
        rotation.astype(jnp.bfloat16), stripe, preferred_element_type=jnp.float32
    ).astype(jnp.bfloat16)
    head_term = lax.dot_general(
        v_full.reshape(-1, DH),
        carried.reshape(-1, DH),
        (((0,), (0,)), ((), ())),
        preferred_element_type=jnp.float32,
    )
    head_rotation_grad = lax.psum(head_term, ("row", "col"))
    return (rotation_grad, head_rotation_grad)


ZS = 4


def kernel(
    token_count,
    hidden,
    target,
    v_weight,
    codes,
    scales,
    head_half,
    rotation,
    rot_grad,
    head_grad,
    hid,
    vf,
    rw,
    part,
    part_own,
    arrived,
    resid,
    g_own,
    g_all,
    rot32,
    vt,
    ut,
    head_sum,
    stage,
    head_term,
    head_in,
    head_out,
    swap_send,
    swap_recv,
    rs_send,
    rs_recv,
    ag_own,
    ag_z,
    ag_x,
    ag_recv,
    g_src,
    g_z,
    g_x,
    g_recv,
    rot_sem,
    out_sem,
    hs_send,
    hs_recv,
    hb_send,
    hb_recv,
):
    r, c = lax.axis_index("row"), lax.axis_index("col")
    z, x = c // 2, c % 2
    me = c * 2 + r
    cols, people = 2 * ZS, 4 * ZS
    width, chans = codes.shape
    half_tokens = hidden.shape[0]
    piece = target.shape[0]
    tile = min(256, chans)
    wtile = min(256, width)

    def copy(src, dst, send, recv, cc, rr):
        return pltpu.make_async_remote_copy(
            src_ref=src,
            dst_ref=dst,
            send_sem=send,
            recv_sem=recv,
            device_id={"col": cc, "row": rr},
            device_id_type=MESH,
        )

    def rot_copy(b):
        return pltpu.make_async_copy(
            rotation.at[:, pl.ds(b * width, width)], rot32.at[b % 2], rot_sem.at[b]
        )

    rot_copy(0).start()
    rot_copy(1).start()

    barrier = pltpu.get_barrier_semaphore()
    for d in range(1, people):
        other = lax.rem(me + d, people)
        pl.semaphore_signal(
            barrier, inc=1, device_id={"col": other // 2, "row": other % 2}, device_id_type=MESH
        )
    pl.semaphore_wait(barrier, people - 1)

    swap_h = copy(hidden, hid.at[r], swap_send.at[0], swap_recv.at[0], c, 1 - r)
    swap_v = copy(v_weight, vf.at[r], swap_send.at[1], swap_recv.at[1], c, 1 - r)
    swap_h.start()

    quantized = (codes[...].astype(F32) * scales[...]).astype(BF16)

    def partial_half(h, tokens):
        product = jnp.dot(tokens[...], quantized, preferred_element_type=F32)
        for i in range(ZS):
            owner = h * ZS + i
            rows = product[i * piece : (i + 1) * piece]
            part[owner] = rows.astype(BF16)

            @pl.when(owner == c)
            def _():
                part_own[...] = rows

        def send(i, carry):
            owner = h * ZS + lax.rem(c + i, ZS)

            @pl.when(owner != c)
            def _():
                copy(
                    part.at[owner], arrived.at[c], rs_send.at[owner], rs_recv.at[c], owner, r
                ).start()

            return carry

        lax.fori_loop(0, ZS, send, 0)

    partial_half(r, hidden)
    swap_h.wait_recv()
    swap_v.start()
    partial_half(1 - r, hid.at[1 - r])
    hid[r] = hidden[...]
    vf[r] = v_weight[...]

    def fold_rotation(b):
        rot_copy(b).wait()

        def body(i, carry):
            at = pl.ds(pl.multiple_of(i * wtile, wtile), wtile)
            ut[b, :, at] = jnp.dot(
                vt[...], rot32[b % 2, :, at].astype(BF16), preferred_element_type=F32
            ).astype(BF16)
            return carry

        lax.fori_loop(0, width // wtile, body, 0)
        if b + 2 < ZS:
            rot_copy(b + 2).start()

    swap_v.wait_recv()
    for k in range(2):
        vt[k * chans : (k + 1) * chans, :] = vf[k].T
    fold_rotation(0)
    fold_rotation(1)
    for k in range(2):
        for n in range(chans // DH):
            cut = slice(n * DH, (n + 1) * DH)
            rw[k, :, cut] = jnp.dot(
                vf[k, :, cut], head_half[...], preferred_element_type=F32
            ).astype(BF16)

    total = part_own[...] - target[...].astype(F32)
    for d in range(1, cols):
        s = lax.rem(c + d, cols)
        copy(part.at[s], arrived.at[s], rs_send.at[s], rs_recv.at[s], s, r).wait_recv()
        total = total + arrived[s].astype(F32)
    resid[c] = (total * (1.0 / math.sqrt(token_count))).astype(BF16)

    def ag_copy(s, sem, cc):
        return copy(resid.at[s], resid.at[s], sem, ag_recv.at[s], cc, r)

    def ag_first(act):
        @pl.when(z < ZS - 1)
        def _():
            act(ag_copy(c, ag_own.at[0], c + 2))

        @pl.when(z > 0)
        def _():
            act(ag_copy(c, ag_own.at[1], c - 2))

        act(ag_copy(c, ag_own.at[2], 2 * z + 1 - x))

    def ag_next(s, up, act):
        if up:

            @pl.when(z < ZS - 1)
            def _():
                act(ag_copy(s, ag_z.at[s], c + 2))

        else:

            @pl.when(z > 0)
            def _():
                act(ag_copy(s, ag_z.at[s], c - 2))

        act(ag_copy(s, ag_x.at[s], 2 * z + 1 - x))

    start = lambda cp: cp.start()
    sent = lambda cp: cp.wait_send()

    ag_first(start)
    fold_rotation(2)
    for d in range(1, ZS):

        @pl.when(z >= d)
        def _():
            s = c - 2 * d
            ag_copy(s, ag_z.at[s], c).wait_recv()
            ag_next(s, True, start)

        @pl.when(z + d < ZS)
        def _():
            s = c + 2 * d
            ag_copy(s, ag_z.at[s], c).wait_recv()
            ag_next(s, False, start)

    fold_rotation(3)
    for zz in range(ZS):
        s = 2 * zz + 1 - x
        ag_copy(s, ag_z.at[s], c).wait_recv()

    home = z // 2
    for n in range(chans // tile):
        cut = slice(n * tile, (n + 1) * tile)
        cot = resid[:, :, cut].reshape(token_count, tile)
        grad = lax.dot_general(
            hid[...].reshape(token_count, width),
            cot,
            (((0,), (0,)), ((), ())),
            preferred_element_type=F32,
        )
        kept = (codes[:, cut] > -8) & (codes[:, cut] < 7)
        g_own[:, cut] = jnp.where(kept, grad, 0.0).astype(BF16)

    def g_copy(src, slot, k, sem, cc, core):
        return copy(src, g_all.at[slot, k], sem, g_recv.at[slot * 2 + k], cc, core)

    mine = lax.rem(c, ZS)

    def g_first(act):
        @pl.when(z < ZS - 1)
        def _():
            act(g_copy(g_own, mine, r, g_src.at[0], c + 2, home))

        @pl.when(z > 0)
        def _():
            act(g_copy(g_own, mine, r, g_src.at[1], c - 2, home))

        act(g_copy(g_own, mine, r, g_src.at[2], 2 * z + 1 - x, home))

        @pl.when(r != home)
        def _():
            act(g_copy(g_own, mine, r, g_src.at[3], c, home))

    g_first(start)

    @pl.when(r == home)
    def _():
        g_all[mine, r] = g_own[...]

    def g_next(zs, k, act):
        slot = lax.rem(2 * zs + x, ZS)
        i = slot * 2 + k
        block = g_all.at[slot, k]

        @pl.when((zs < z) & (z < ZS - 1))
        def _():
            act(g_copy(block, slot, k, g_z.at[i], c + 2, r))

        @pl.when((zs > z) & (z > 0))
        def _():
            act(g_copy(block, slot, k, g_z.at[i], c - 2, r))

        crosses = zs != z
        if k == 1:
            crosses = crosses & (zs != end)

        @pl.when(crosses)
        def _():
            act(g_copy(block, slot, k, g_x.at[i], 2 * z + 1 - x, r))

    def g_beside(act):
        slot = lax.rem(2 * end + 1 - x, ZS)
        i = slot * 2 + 1

        @pl.when((r == 0) & (z < ZS - 1))
        def _():
            act(g_copy(g_all.at[slot, 1], slot, 1, g_z.at[i], c + 2, r))

        @pl.when((r == 1) & (z > 0))
        def _():
            act(g_copy(g_all.at[slot, 1], slot, 1, g_z.at[i], c - 2, r))

    end = (ZS - 1) * r
    near = jnp.clip(z, 2 * r, 2 * r + 1)
    far = 4 * r + 1 - near

    def out_copy(slot, n):
        return pltpu.make_async_copy(
            stage.at[n], rot_grad.at[:, pl.ds(pl.multiple_of(slot * width, 128), width)], out_sem.at[n]
        )

    def rotation_work(slot, n):
        if n >= 2:
            out_copy(slot, n % 2).wait()

        def outputs(i, carry):
            rows = pl.ds(pl.multiple_of(i * wtile, wtile), wtile)
            contract = (((1,), (1,)), ((), ()))
            stage[n % 2, :, rows] = lax.dot_general(
                rw[0], g_all[slot, 0, rows, :], contract, preferred_element_type=F32
            ) + lax.dot_general(
                rw[1], g_all[slot, 1, rows, :], contract, preferred_element_type=F32
            )
            return carry

        lax.fori_loop(0, width // wtile, outputs, 0)
        out_copy(slot, n % 2).start()

    def head_work(slot):
        pairs = chans // (2 * DH)

        def heads(i, carry):
            k = i // pairs
            rows = pl.ds(pl.multiple_of(i * 2 * DH, 2 * DH), 2 * DH)
            cut = pl.ds(pl.multiple_of(lax.rem(i, pairs) * 2 * DH, 2 * DH), 2 * DH)
            head_sum[...] += jnp.dot(
                ut[slot, rows, :], g_all[slot, k, :, cut], preferred_element_type=F32
            )
            return carry

        lax.fori_loop(0, 2 * pairs, heads, 0)

    def work(slot, n):
        rotation_work(slot, n)
        head_work(slot)

    def g_wait(slot, k):
        copy(g_own, g_all.at[slot, k], g_src.at[0], g_recv.at[slot * 2 + k], c, r).wait_recv()

    near_own, far_own = lax.rem(2 * near + x, ZS), lax.rem(2 * far + x, ZS)
    near_off, far_off = lax.rem(2 * near + 1 - x, ZS), lax.rem(2 * far + 1 - x, ZS)
    early = z + (ZS - 1) * r == ZS - 1

    head_sum[...] = jnp.zeros_like(head_sum)
    for k in range(2):

        @pl.when((near != z) | (r != k))
        def _():
            g_wait(near_own, k)

        g_next(near, k, start)
    work(near_own, 0)

    @pl.when(early)
    def _():
        g_wait(near_off, 0)
        g_wait(near_off, 1)
        work(near_off, 1)

    for k in range(2):
        g_wait(far_own, k)
        g_next(far, k, start)
    g_wait(lax.rem(2 * end + 1 - x, ZS), 1)
    g_beside(start)

    @pl.when(jnp.logical_not(early))
    def _():
        g_wait(near_off, 0)

        @pl.when(near != end)
        def _():
            g_wait(near_off, 1)

        work(near_off, 1)

    work(far_own, 2)
    g_wait(far_off, 0)

    @pl.when(far != end)
    def _():
        g_wait(far_off, 1)

    head_work(far_off)

    term = head_sum[:DH, :DH] + head_sum[DH:, DH:]
    share = DH // people
    head_term[...] = term.reshape(people, share, DH)

    def hs_copy(d):
        other = lax.rem(me + d, people)
        return copy(
            head_term.at[other],
            head_in.at[me],
            hs_send.at[other],
            hs_recv.at[me],
            other // 2,
            other % 2,
        )

    def hb_copy(d):
        other = lax.rem(me + d, people)
        return copy(
            head_out.at[me],
            head_out.at[me],
            hb_send.at[other],
            hb_recv.at[me],
            other // 2,
            other % 2,
        )

    for d in range(1, people):
        hs_copy(d).start()
    rotation_work(far_off, 3)
    total = head_term[me]
    for d in range(1, people):
        s = lax.rem(me + d, people)
        copy(head_in.at[s], head_in.at[s], hs_send.at[s], hs_recv.at[s], c, r).wait_recv()
        total = total + head_in[s]
    head_out[me] = total
    for d in range(1, people):
        hb_copy(d).start()
    for d in range(1, people):
        s = lax.rem(me + d, people)
        copy(head_out.at[s], head_out.at[s], hb_send.at[s], hb_recv.at[s], c, r).wait_recv()
    head_grad[...] = head_out[...].reshape(DH, DH)

    for d in range(1, people):
        hs_copy(d).wait_send()
        hb_copy(d).wait_send()
    swap_h.wait_send()
    swap_v.wait_send()
    for d in range(1, cols):
        s = lax.rem(c + d, cols)
        copy(part.at[s], arrived.at[c], rs_send.at[s], rs_recv.at[c], s, r).wait_send()
    ag_first(sent)
    for d in range(1, ZS):

        @pl.when(z >= d)
        def _():
            ag_next(c - 2 * d, True, sent)

        @pl.when(z + d < ZS)
        def _():
            ag_next(c + 2 * d, False, sent)

    g_first(sent)
    for zs in (near, far):
        for k in range(2):
            g_next(zs, k, sent)
    g_beside(sent)
    out_copy(0, 0).wait()
    out_copy(0, 1).wait()


def on_grid(hidden, target, v_weight, codes, exponents, rotation, head_rotation):
    width, chans = codes.shape
    piece = target.shape[0]
    cols, people = 2 * ZS, 4 * ZS
    token_count = 2 * hidden.shape[0]
    scales = jnp.exp2(-exponents.astype(F32))[None, :]
    head_half = head_rotation.astype(BF16)
    vmem = pl.BlockSpec(memory_space=pltpu.VMEM)
    anywhere = pl.BlockSpec(memory_space=pl.ANY)
    dma = pltpu.SemaphoreType.DMA
    return pl.pallas_call(
        functools.partial(kernel, token_count),
        out_shape=(
            jax.ShapeDtypeStruct(rotation.shape, F32),
            jax.ShapeDtypeStruct((DH, DH), F32),
        ),
        in_specs=[vmem] * 6 + [anywhere],
        out_specs=(anywhere, vmem),
        scratch_shapes=[
            pltpu.VMEM((2,) + hidden.shape, BF16),
            pltpu.VMEM((2, width, chans), BF16),
            pltpu.VMEM((2, width, chans), BF16),
            pltpu.VMEM((cols, piece, chans), BF16),
            pltpu.VMEM((piece, chans), F32),
            pltpu.VMEM((cols, piece, chans), BF16),
            pltpu.VMEM((cols, piece, chans), BF16),
            pltpu.VMEM((width, chans), BF16),
            pltpu.VMEM((ZS, 2, width, chans), BF16),
            pltpu.VMEM((2, width, width), F32),
            pltpu.VMEM((2 * chans, width), BF16),
            pltpu.VMEM((ZS, 2 * chans, width), BF16),
            pltpu.VMEM((2 * DH, 2 * DH), F32),
            pltpu.VMEM((2, width, width), F32),
            pltpu.VMEM((people, DH // people, DH), F32),
            pltpu.VMEM((people, DH // people, DH), F32),
            pltpu.VMEM((people, DH // people, DH), F32),
            dma((2,)),
            dma((2,)),
            dma((cols,)),
            dma((cols,)),
            dma((3,)),
            dma((cols,)),
            dma((cols,)),
            dma((cols,)),
            dma((4,)),
            dma((cols,)),
            dma((cols,)),
            dma((cols,)),
            dma((ZS,)),
            dma((2,)),
            dma((people,)),
            dma((people,)),
            dma((people,)),
            dma((people,)),
        ],
        compiler_params=pltpu.CompilerParams(
            collective_id=0, has_side_effects=True, vmem_limit_bytes=62 * 1024 * 1024
        ),
    )(hidden, target, v_weight, codes, scales, head_half, rotation)


def solution(mesh):
    in_specs = (
        P(("parts", "row"), "col"),
        P(("parts", "col"), "row"),
        P(("parts", "col"), "row"),
        P(("parts", "col"), "row"),
        P(("parts", "row")),
        P("col", "row"),
        P("parts", None),
    )
    out_specs = (P(("parts", "col"), "row"), P("parts", None))
    routed = mesh.shape["col"] == 2 * ZS and mesh.shape["row"] == 2
    return jax.shard_map(
        on_grid if routed else on_device,
        mesh=mesh,
        in_specs=in_specs,
        out_specs=out_specs,
        check_vma=False,
    )
```
